1024 devices in a mesh: gx: 8 (over x, y_lo), gy: 8 (over y_hi, core), gz: 16 (over z).
Axes of the slice: x: 4, y: 8 (y_hi: 4, y_lo: 2; y = y_hi * 2 + y_lo), z: 16, core: 2. Of those that a mesh axis runs over, the one named last changes fastest.
Arguments:
- spectrum: float32 [3, 2, 64, 64, 2048], P(None, None, ('gy', 'gx'), None, 'gz'), may hold values from -0.3125 to 0.3125
- theta: float32 [64, 64, 8192], P('gy', 'gz', 'gx'), may hold values from -6 to 6
- section_sum: float32 [64, 64, 8192], P('gy', 'gz', 'gx'), may hold values from -6 to 6
- seg_offset: int32 [8], replicated, may hold values from 0 to 3328, as said below
- seg_length: int32 [8], replicated, may hold values from 256 to 768, as said below
- stencil_index: int32 [8, 8192], replicated, may hold values from 0 to 767, as said below
- stencil_weight: float32 [8, 8192], replicated, may hold values from 0 to 0.25
Outputs:
- theta_next: float32 [64, 64, 8192], P('gy', 'gz', 'gx')
- section_next: float32 [64, 64, 8192], P('gy', 'gz', 'gx')
The draws below stay inside these ranges and needn't reach their ends.
Inputs may be any that keep to these rules, and one draw needn't show every extreme that they name: `seg_length`: some block's segment holds exactly 768 cells. For every block i, seg_offset[i] + 768 <= 4096. `stencil_index`: positions count from the start of the segment of the scalar cell's x block; taps at or past that segment's length are padding.
All inputs are finite; a program needn't handle non-finite values.
Results may differ from the reference program's by a relative error of at most 0.00005.
Values sent between devices are 32-bit elements; how exact they have to be, the bound alone decides.
No kernel may reach another device: no remote copies, remote signals or barrier semaphores. Data moves between devices by JAX's collectives and lax.ppermute only.
A program may use at most 64 MiB of HBM per device.

```python
import jax
import jax.numpy as jnp
from jax import lax

TAPS = 8
NVX = 4096
K = 2048
NSX = 8192
NSY = 64
NSZ = 64
MAXSEG = 768
N_GX = 8


def segments_drawn(key):
    base_key = jax.random.fold_in(key, 7)
    length_key, longest_key = jax.random.split(base_key)
    lengths = jax.random.randint(length_key, (N_GX,), MAXSEG // 3, MAXSEG + 1, dtype=jnp.int32)
    longest = jax.random.randint(longest_key, (), 0, N_GX, dtype=jnp.int32)
    block_number = jnp.arange(N_GX, dtype=jnp.int32)
    lengths = jnp.where(block_number == longest, MAXSEG, lengths)
    centers = block_number * (NVX // N_GX) + NVX // (2 * N_GX)
    offsets = jnp.clip(centers - lengths // 2, 0, NVX - MAXSEG)
    return (offsets.astype(jnp.int32), lengths.astype(jnp.int32))


def draw_seg_offset(key, part):
    return segments_drawn(key)[0]


def draw_seg_length(key, part):
    return segments_drawn(key)[1]


def draw_stencil_index(key, part):
    offsets, lengths = segments_drawn(key)
    block_cells = NSX // N_GX
    cell_index = jnp.arange(NSX, dtype=jnp.int32)
    within = cell_index % block_cells
    owner_block = cell_index // block_cells
    owner_length = jnp.sum(jnp.where(owner_block[:, None] == jnp.arange(N_GX, dtype=jnp.int32)[None, :], lengths[None, :], 0), axis=1)
    jitter = jax.random.randint(jax.random.fold_in(key, 13), (NSX,), 0, 3, dtype=jnp.int32)
    anchor = within * owner_length // block_cells + jitter
    tap_shift = jnp.arange(TAPS, dtype=jnp.int32)[:, None] - TAPS // 2 + 1
    return jnp.clip(anchor[None, :] + tap_shift, 0, MAXSEG - 1).astype(jnp.int32)


def level_of(rng, extent, shards, least, top_value):
    def one(position, shards_of):
        heights = jax.random.uniform(jax.random.fold_in(jax.random.fold_in(rng, 6), position), (shards_of,), jnp.float32, least / len(shards), top_value / len(shards))
        return jnp.repeat(jnp.exp(heights), extent[position] // shards_of).reshape((-1,) + (1,) * (len(extent) - position - 1))

    factor_of = one(*shards[0])
    for cut in shards[1:]:
        factor_of = factor_of * one(*cut)
    return factor_of


def scatter_about(rng, extent, spread, most, cuts=(), kind=jnp.bfloat16):
    entries = jax.random.normal(rng, extent, jnp.float32) * spread
    if len(cuts) > 0:
        entries = level_of(rng, extent, cuts, -0.22, 0.18) * entries
    return jnp.clip(entries, min=-most, max=most).astype(kind)


def setup_inputs(seed: int = 0) -> dict:
    seeds = jax.random.split(jax.random.key(seed), 8)
    return {
        "spectrum": scatter_about(seeds[0], (3, 2, NSY, NSZ, K), ((2.0 / NVX) ** 0.5), 0.3125, ((2, 64), (4, 16)), jnp.float32),
        "theta": scatter_about(seeds[1], (NSY, NSZ, NSX), 1.0, 6.0, ((0, 8), (1, 16), (2, 8)), jnp.float32),
        "section_sum": scatter_about(seeds[2], (NSY, NSZ, NSX), 0.5, 6.0, ((0, 8), (1, 16), (2, 8)), jnp.float32),
        "seg_offset": draw_seg_offset(jax.random.fold_in(seeds[7], 71), 0),
        "seg_length": draw_seg_length(jax.random.fold_in(seeds[7], 71), 0),
        "stencil_index": draw_stencil_index(jax.random.fold_in(seeds[7], 71), 0),
        "stencil_weight": jnp.clip(jax.random.uniform(seeds[6], (TAPS, NSX), jnp.float32, 0.0, 0.25), 0.0, 0.25),
    }


first_coeffs = (0.8, -0.2, 4.0 / 105.0, -1.0 / 280.0)
second_coeffs = (1.6, -0.2, 8.0 / 315.0, -1.0 / 560.0)
center_coeff = -205.0 / 72.0
diffusivity = 0.15
time_step = 0.4
section_keep = -5.0 / 9.0
section_gain = 15.0 / 16.0


def reference(spectrum, theta, section_sum, seg_offset, seg_length, stencil_index, stencil_weight):
    line_length = 2 * spectrum.shape[-1]
    scalar_cells = theta.shape[2]
    block_cells = scalar_cells // N_GX
    block_of = (jnp.arange(scalar_cells, dtype=jnp.int32) // block_cells).astype(jnp.int32)
    start_of = seg_offset[block_of]
    length_of = seg_length[block_of]
    absolute = (start_of[None, :] + stencil_index).astype(jnp.int32)
    live_weight = jnp.where(stencil_index < length_of[None, :], stencil_weight, 0.0)
    theta_cycle = jnp.concatenate([theta[-4:], theta, theta[:4]], axis=0)

    def one_row(row_index):
        coeffs = spectrum[:, 0, row_index] + 1j * spectrum[:, 1, row_index]
        velocity = line_length * jnp.real(jnp.fft.ifft(coeffs, n=line_length, axis=-1))
        carried = jnp.zeros((3, theta.shape[1], scalar_cells), jnp.float32)
        for tap_number in range(stencil_index.shape[0]):
            carried = carried + live_weight[tap_number] * jnp.take(velocity, absolute[tap_number], axis=-1)
        slab = lax.dynamic_slice_in_dim(theta_cycle, row_index, 9, 0)
        center = slab[4]
        grad_x = jnp.zeros_like(center)
        grad_y = jnp.zeros_like(center)
        grad_z = jnp.zeros_like(center)
        laplace = 3.0 * center_coeff * center
        for reach in range(1, 5):
            ahead_x = jnp.roll(center, -reach, axis=1)
            behind_x = jnp.roll(center, reach, axis=1)
            ahead_z = jnp.roll(center, -reach, axis=0)
            behind_z = jnp.roll(center, reach, axis=0)
            ahead_y = slab[4 + reach]
            behind_y = slab[4 - reach]
            first = first_coeffs[reach - 1]
            second = second_coeffs[reach - 1]
            grad_x = grad_x + first * (ahead_x - behind_x)
            grad_y = grad_y + first * (ahead_y - behind_y)
            grad_z = grad_z + first * (ahead_z - behind_z)
            laplace = laplace + second * (ahead_x + behind_x + ahead_y + behind_y + ahead_z + behind_z)
        change = -(carried[0] * grad_x + carried[1] * grad_y + carried[2] * grad_z) + diffusivity * laplace
        register = lax.dynamic_index_in_dim(section_sum, row_index, 0, keepdims=False)
        section_next = section_keep * register + time_step * change
        return center + section_gain * section_next, section_next

    theta_next, section_next = lax.map(one_row, jnp.arange(theta.shape[0], dtype=jnp.int32))
    return theta_next, section_next
```

```python
import functools
import math

import jax
import jax.numpy as jnp
import numpy as np
from jax import lax
from jax.experimental import pallas as pl
from jax.experimental.pallas import tpu as pltpu
from jax.sharding import PartitionSpec as P

first_coeffs = (0.8, -0.2, 4.0 / 105.0, -1.0 / 280.0)
second_coeffs = (1.6, -0.2, 8.0 / 315.0, -1.0 / 560.0)
center_coeff = -205.0 / 72.0
diffusivity = 0.15
time_step = 0.4
section_keep = -5.0 / 9.0
section_gain = 15.0 / 16.0

LANES = 128
LOW = 32
SEGMENT = 6
WINDOW = 8
VMEM_LIMIT = 16 * 1024 * 1024


def halves(values):
    high = values.astype(jnp.bfloat16)
    return high, (values - high.astype(jnp.float32)).astype(jnp.bfloat16)


def numpy_halves(values):
    values = values.astype(np.float32)
    high = values.astype(jnp.bfloat16)
    return high, (values - high.astype(np.float32)).astype(jnp.bfloat16)


def dot(a, b):
    return jnp.dot(a, b, preferred_element_type=jnp.float32)


@functools.cache
def tables():
    j = np.arange(LANES)
    h, g = np.meshgrid(np.arange(4), np.arange(16), indexing="ij")
    angle = 2 * math.pi * (((4 * g + h)[:, :, None] * j) % LANES) / LANES
    real_rows = np.concatenate([np.cos(angle), np.sin(angle)], -1)
    imag_rows = np.concatenate([-np.sin(angle), np.cos(angle)], -1)
    first = np.stack([real_rows, imag_rows], 1).reshape(LANES, 2 * LANES)
    first_high, first_low = numpy_halves(first)
    low = np.arange(LOW)
    twist = 2 * math.pi * (low[:, None] * j[None, :]) / (LOW * LANES)
    twiddle = np.stack([np.cos(twist), np.sin(twist)]).astype(np.float32)
    m = np.arange(LOW)[:, None, None] + np.arange(WINDOW)[:, None]
    last_angle = 2 * math.pi * ((m * low) % LOW) / LOW
    last = np.concatenate([np.cos(last_angle), -np.sin(last_angle)], -1)
    last_high, last_low = (t.astype(np.float32) for t in numpy_halves(last))
    last_all = np.concatenate([last_high, last_low, last_high], -1)
    return np.concatenate([first_high, first_high, first_low], 0), twiddle, last_all


def pack_kernel(spectrum_ref, theta_ref, out_ref, low_ref, high_ref, got, packed, sems):
    groups, dests, rows = 2, out_ref.shape[0], theta_ref.shape[0]
    count = dests // groups
    heads = [
        pltpu.make_async_copy(
            spectrum_ref.at[:, pl.ds(4 * count * group, 4 * count), :],
            got.at[:, pl.ds(4 * count * group, 4 * count), :],
            sems.at[group],
        )
        for group in range(groups)
    ]
    tails = [
        pltpu.make_async_copy(
            packed.at[pl.ds(count * group, count)],
            out_ref.at[pl.ds(count * group, count)],
            sems.at[groups + group],
        )
        for group in range(groups)
    ]
    sides = [
        pltpu.make_async_copy(theta_ref.at[pl.ds(0, 4)], low_ref, sems.at[2 * groups]),
        pltpu.make_async_copy(theta_ref.at[pl.ds(rows - 4, 4)], high_ref, sems.at[2 * groups + 1]),
    ]
    for copy in heads + sides:
        copy.start()
    for group in range(groups):
        heads[group].wait()
        for dest in range(count * group, count * (group + 1)):
            for part in range(6):
                packed[dest, 4 * part : 4 * part + 4, :] = got[part, 4 * dest : 4 * dest + 4, :]
        tails[group].start()
    for copy in tails + sides:
        copy.wait()


def edges_of(theta_ref):
    spot = lax.broadcasted_iota(jnp.int32, (8, LANES), 1)
    edges = jnp.zeros((8, LANES), jnp.float32)
    cells = theta_ref.shape[2]
    for z in range(4):
        tail = pltpu.roll(theta_ref[:, z, cells - LANES :], (8 * z + 4) % LANES, 1)
        head = pltpu.roll(theta_ref[:, z, :LANES], 8 * z + 4, 1)
        edges = jnp.where((spot >= 8 * z) & (spot < 8 * z + 4), tail, edges)
        edges = jnp.where((spot >= 8 * z + 4) & (spot < 8 * z + 8), head, edges)
    return edges


def setup_kernel(
    offset_hbm, theta_hbm, last_hbm, first_hbm, twiddle_hbm,
    left_ref, turn_ref, edges_ref, first_ref, twiddle_ref,
    offset, theta, last, sems,
):
    moves = ((offset_hbm, offset), (theta_hbm, theta), (last_hbm, last))
    moves += ((first_hbm, first_ref), (twiddle_hbm, twiddle_ref))
    copies = [
        pltpu.make_async_copy(source, target, sems.at[number])
        for number, (source, target) in enumerate(moves)
    ]
    for copy in copies:
        copy.start()
    for copy in copies:
        copy.wait()
    blocks = left_ref.shape[0] // WINDOW
    left = [last[offset[block] // LANES] for block in range(blocks)]
    left_ref[...] = jnp.concatenate(left, 0).astype(jnp.bfloat16)
    lane = lax.broadcasted_iota(jnp.int32, (1, LANES), 1)
    for block in range(blocks):
        turn_ref[block : block + 1, :] = jnp.where(lane < offset[block] % LANES, 1.0, 0.0)
    edges_ref[...] = edges_of(theta)


def fill_matrix(start, length, index_ref, weight_ref, matrix, matrix_ref, sems):
    rows = lax.broadcasted_iota(jnp.int32, (8, LANES), 0)
    taps = index_ref.shape[0]
    copies = []
    for pair in range(matrix.shape[0]):
        for side in range(2):
            lanes = slice((2 * pair + side) * LANES, (2 * pair + side + 1) * LANES)
            index = index_ref[:, lanes]
            weight = jnp.where(index < length, weight_ref[:, lanes], 0.0)
            inner = lax.rem(index + start, LANES)
            spots = [jnp.broadcast_to(inner[t : t + 1], (8, LANES)) for t in range(taps)]
            parts = []
            for m in range(SEGMENT):
                part = jnp.where(index // LANES == m, weight, 0.0)
                parts.append([jnp.broadcast_to(part[t : t + 1], (8, LANES)) for t in range(taps)])

            def step(number, carry, side=side, pair=pair, spots=spots, parts=parts):
                near = [rows + 16 * number, rows + (16 * number + 8)]
                hits = [[near[half] == spots[t] for t in range(taps)] for half in range(2)]
                for m in range(SEGMENT):
                    total = []
                    for half in range(2):
                        terms = [jnp.where(hits[half][t], parts[m][t], 0.0) for t in range(taps)]
                        while len(terms) > 1:
                            terms = [a + b for a, b in zip(terms[::2], terms[1::2], strict=True)]
                        total.append(terms[0])
                    high, low = halves(jnp.concatenate(total, 0))
                    at = pl.ds(pl.multiple_of(LANES * m + 16 * number, 16), 16)
                    matrix[pair, 0, at, side * LANES : (side + 1) * LANES] = high
                    matrix[pair, 1, at, side * LANES : (side + 1) * LANES] = low
                return carry

            lax.fori_loop(0, LANES // 16, step, 0)
        copies.append(pltpu.make_async_copy(matrix.at[pair], matrix_ref.at[pair], sems.at[pair]))
        copies[-1].start()
    return copies


def transform_kernel(
    got_ref, first_ref, twiddle_ref, left_ref, turn_ref, edges_ref, *after_and_out
):
    out_ref = after_and_out[-1]
    lane = lax.broadcasted_iota(jnp.int32, (LOW, LANES), 1) // LOW
    pieces = []
    for comp in range(3):
        rows = [
            got_ref[pl.ds(comp * 8 + part * 4 + z, 16, stride=24), :]
            for z in range(4)
            for part in range(2)
        ]
        turned = jnp.concatenate(rows, 0).T
        for z in range(4):
            piece = jnp.zeros((LOW, LANES), jnp.float32)
            for h in range(4):
                moved = turned[LOW * h : LOW * (h + 1), :]
                if h != z:
                    moved = pltpu.roll(moved, (LOW * (h - z)) % LANES, 1)
                piece = jnp.where(lane == h, moved, piece)
            pieces.append(piece)
    high, low = halves(jnp.concatenate(pieces, 0))
    done = dot(jnp.concatenate([high, low], 1), first_ref[: 2 * LANES, :]) + dot(
        high, first_ref[2 * LANES :, :]
    )
    cosine, sine = twiddle_ref[0], twiddle_ref[1]
    right = []
    for line in range(12):
        real = done[LOW * line : LOW * (line + 1), :LANES]
        imag = done[LOW * line : LOW * (line + 1), LANES:]
        high, low = halves(
            jnp.concatenate([real * cosine - imag * sine, real * sine + imag * cosine], 0)
        )
        right.append(jnp.concatenate([high, high, low], 0))
    lines = dot(left_ref[...], jnp.concatenate(right, 1))
    for block in range(out_ref.shape[0]):
        turned = jnp.broadcast_to(turn_ref[block : block + 1, :], (WINDOW, LANES)) > 0.5
        for line in range(12):
            cells = lines[WINDOW * block : WINDOW * (block + 1), line * LANES : (line + 1) * LANES]
            out_ref[block, line] = jnp.where(turned, pltpu.roll(cells, WINDOW - 1, 0), cells)
    for block in range(out_ref.shape[0]):
        for y in range(8):
            out_ref[block, y, WINDOW - 1 :, :] = edges_ref[y : y + 1]


def local_kernel(
    z_low_ref, z_high_ref, y_low_ref, y_high_ref,
    theta_hbm, sum_hbm, offset_hbm, length_hbm, index_hbm, weight_hbm, after_ref,
    out_ref, matrix_ref,
    theta, sums, offset, length, index, weight, matrix, sems, out_sems,
):
    block = lax.axis_index("gx")
    cells = theta.shape[2]
    mine = pl.ds(pl.multiple_of(block * cells, LANES), cells)
    moves = ((offset_hbm, offset), (length_hbm, length))
    moves += ((index_hbm.at[:, mine], index), (weight_hbm.at[:, mine], weight))
    moves += ((theta_hbm, theta), (sum_hbm, sums))
    copies = [
        pltpu.make_async_copy(source, target, sems.at[number])
        for number, (source, target) in enumerate(moves)
    ]
    for copy in copies:
        copy.start()
    for copy in copies[:4]:
        copy.wait()
    tails = fill_matrix(offset[block], length[block], index, weight, matrix, matrix_ref, out_sems)
    for copy in copies[4:]:
        copy.wait()
    stencil(theta, sums, z_low_ref, z_high_ref, y_low_ref, y_high_ref, out_ref)
    for copy in tails:
        copy.wait()


def stencil(theta_ref, sum_ref, z_low_ref, z_high_ref, y_low_ref, y_high_ref, out_ref):
    cells = theta_ref.shape[2]
    lane = lax.broadcasted_iota(jnp.int32, (8, cells), 1)
    planes = [ref[:, z, :] for ref in (z_low_ref, theta_ref, z_high_ref) for z in range(4)]
    for z in range(4):
        here = planes[4 + z]
        column = jnp.concatenate([y_low_ref[:, z, :], here, y_high_ref[:, z, :]], 0)
        grad_x = jnp.zeros_like(here)
        grad_y = jnp.zeros_like(here)
        grad_z = jnp.zeros_like(here)
        laplace = 3.0 * center_coeff * here
        for reach in range(1, 5):
            first = -time_step * first_coeffs[reach - 1]
            ahead_x = jnp.where(lane < cells - reach, pltpu.roll(here, cells - reach, 1), 0.0)
            behind_x = jnp.where(lane >= reach, pltpu.roll(here, reach, 1), 0.0)
            ahead_y = column[4 + reach : 12 + reach]
            behind_y = column[4 - reach : 12 - reach]
            ahead_z = planes[4 + z + reach]
            behind_z = planes[4 + z - reach]
            grad_x = grad_x + first * (ahead_x - behind_x)
            grad_y = grad_y + first * (ahead_y - behind_y)
            grad_z = grad_z + first * (ahead_z - behind_z)
            laplace = laplace + second_coeffs[reach - 1] * (
                (ahead_x + behind_x) + (ahead_y + behind_y) + (ahead_z + behind_z)
            )
        out_ref[0, z] = grad_x
        out_ref[1, z] = grad_y
        out_ref[2, z] = grad_z
        out_ref[3, z] = section_keep * sum_ref[:, z, :] + (time_step * diffusivity) * laplace
        out_ref[4, z] = here


def combine_kernel(
    got_ref, matrix_hbm, local_ref, theta_ref, section_ref, matrix_ref, sems
):
    copies = [
        pltpu.make_async_copy(matrix_hbm.at[pair], matrix_ref.at[pair], sems.at[pair])
        for pair in range(matrix_ref.shape[0])
    ]
    for copy in copies:
        copy.start()
    block = lax.axis_index("gx")
    blocks = got_ref.shape[0] // (12 * WINDOW)
    cells = local_ref.shape[3]
    rows = [
        jnp.concatenate(
            [
                got_ref[pl.ds(WINDOW * line + m, blocks, stride=12 * WINDOW), :]
                for line in range(12)
            ],
            0,
        )
        for m in range(SEGMENT)
    ]
    high, low = halves(jnp.concatenate(rows, 1))
    both = jnp.concatenate([high, low], 0)
    count = high.shape[0]

    def halo_of(source):
        return got_ref[pl.ds(source * 12 * WINDOW + WINDOW - 1, 8, stride=WINDOW), :]

    before = halo_of(lax.rem(block + blocks - 1, blocks))
    after = halo_of(lax.rem(block + 1, blocks))
    lane = lax.broadcasted_iota(jnp.int32, (8, LANES), 1)
    width = 2 * LANES
    for tile in range(cells // width):
        lanes = slice(tile * width, (tile + 1) * width)
        copies[tile].wait()
        twice = dot(both, matrix_ref[tile, 0])
        carried = twice[:count] + twice[count:] + dot(high, matrix_ref[tile, 1])
        for z in range(4):
            grad_x = local_ref[0, z, :, lanes]
            base = local_ref[3, z, :, lanes]
            if tile == 0 or (tile + 1) * width == cells:
                more_grad = jnp.zeros((8, LANES), jnp.float32)
                more_base = jnp.zeros((8, LANES), jnp.float32)
                for reach in range(1, 5):
                    if tile == 0:
                        moved = pltpu.roll(before, (LANES - 4 - 8 * z + reach) % LANES, 1)
                        halo = jnp.where(lane < reach, moved, 0.0)
                        sign = 1.0
                    else:
                        moved = pltpu.roll(after, (LANES - 4 - 8 * z - reach) % LANES, 1)
                        halo = jnp.where(lane >= LANES - reach, moved, 0.0)
                        sign = -1.0
                    more_grad = more_grad + (sign * time_step * first_coeffs[reach - 1]) * halo
                    more_base = (
                        more_base + (time_step * diffusivity * second_coeffs[reach - 1]) * halo
                    )
                none = jnp.zeros((8, LANES), jnp.float32)
                order = (lambda v: [v, none]) if tile == 0 else (lambda v: [none, v])
                grad_x = grad_x + jnp.concatenate(order(more_grad), 1)
                base = base + jnp.concatenate(order(more_base), 1)
            section = (
                base
                + carried[8 * z : 8 * z + 8] * grad_x
                + carried[32 + 8 * z : 40 + 8 * z] * local_ref[1, z, :, lanes]
                + carried[64 + 8 * z : 72 + 8 * z] * local_ref[2, z, :, lanes]
            )
            section_ref[:, z, lanes] = section
            theta_ref[:, z, lanes] = local_ref[4, z, :, lanes] + section_gain * section


def f32(*shape):
    return jax.ShapeDtypeStruct(shape, jnp.float32)


def bf16(*shape):
    return jax.ShapeDtypeStruct(shape, jnp.bfloat16)


VMEM = pl.BlockSpec(memory_space=pltpu.VMEM)
HBM = pl.BlockSpec(memory_space=pltpu.HBM)
ANY = pl.BlockSpec(memory_space=pl.ANY)


def in_hbm(array):
    return pltpu.with_memory_space_constraint(array, pltpu.HBM)


def run(kernel, name, in_specs, outs, scratch=()):
    return pl.pallas_call(
        kernel,
        out_shape=tuple(shape for shape, _ in outs),
        in_specs=in_specs,
        out_specs=tuple(spec for _, spec in outs),
        scratch_shapes=scratch,
        compiler_params=pltpu.CompilerParams(vmem_limit_bytes=VMEM_LIMIT),
        cost_estimate=pl.CostEstimate(flops=4 * 10**9, bytes_accessed=4 * 10**6, transcendentals=0),
        name=name,
    )


def neighbours(edge_low, edge_high, axis):
    count = lax.axis_size(axis)
    up = [(i, (i + 1) % count) for i in range(count)]
    return lax.ppermute(edge_high, axis, up), lax.ppermute(edge_low, axis, [(b, a) for a, b in up])


def body(spectrum, theta, section_sum, seg_offset, seg_length, stencil_index, stencil_weight):
    blocks, depth = lax.axis_size("gx"), lax.axis_size("gz")
    rows_count, layers, cells = theta.shape
    taps = stencil_index.shape[0]
    first, twiddle, last = (jnp.asarray(t) for t in tables())
    vmem, smem, dma = pltpu.VMEM, pltpu.SMEM, pltpu.SemaphoreType.DMA

    edge = f32(4, layers, cells)
    packed, y_first, y_last = run(
        pack_kernel,
        "pack",
        [HBM, HBM],
        [(f32(depth, 24, LANES), HBM), (edge, HBM), (edge, HBM)],
        [vmem((6, 4 * depth, LANES), jnp.float32), vmem((depth, 24, LANES), jnp.float32), dma((6,))],
    )(in_hbm(spectrum.reshape(6, 4 * depth, LANES)), in_hbm(theta))
    columns = lax.all_to_all(packed, "gz", split_axis=0, concat_axis=0, tiled=True)
    z_low, z_high = neighbours(theta, theta, "gz")
    y_low, y_high = neighbours(y_first, y_last, "gy")
    left, turn, edges, first, twiddle = run(
        setup_kernel,
        "setup",
        [HBM] * 5,
        [
            (bf16(blocks * WINDOW, last.shape[2]), VMEM),
            (f32(blocks, LANES), VMEM),
            (f32(8, LANES), VMEM),
            (bf16(*first.shape), VMEM),
            (f32(*twiddle.shape), VMEM),
        ],
        [smem((blocks,), jnp.int32), vmem(theta.shape, jnp.float32), vmem(last.shape, jnp.float32)]
        + [dma((5,))],
    )(seg_offset, theta, last, first, twiddle)
    (pieces,) = run(
        transform_kernel,
        "transform",
        [VMEM] * 6 + [ANY] * 4,
        [(f32(blocks, 12, WINDOW, LANES), VMEM)],
    )(
        columns.reshape(depth * 24, LANES), first, twiddle, left, turn, edges,
        z_low, z_high, y_low, y_high,
    )
    arrived = lax.all_to_all(pieces, "gx", split_axis=0, concat_axis=0, tiled=True)
    matrix_shape = (cells // (2 * LANES), 2, SEGMENT * LANES, 2 * LANES)
    local, matrix = run(
        local_kernel,
        "local",
        [VMEM] * 4 + [HBM] * 6 + [ANY],
        [(f32(5, layers, rows_count, cells), VMEM), (pltpu.HBM(matrix_shape, jnp.bfloat16), HBM)],
        [vmem(theta.shape, jnp.float32), vmem(theta.shape, jnp.float32)]
        + [smem((blocks,), jnp.int32), smem((blocks,), jnp.int32)]
        + [vmem((taps, cells), jnp.int32), vmem((taps, cells), jnp.float32)]
        + [vmem(matrix_shape, jnp.bfloat16), dma((6,)), dma((matrix_shape[0],))],
    )(
        z_low, z_high, y_low, y_high,
        theta, section_sum, seg_offset, seg_length, stencil_index, stencil_weight, pieces,
    )
    matrix = in_hbm(matrix)
    return run(
        combine_kernel,
        "combine",
        [VMEM, HBM, VMEM],
        [(f32(*theta.shape), VMEM), (f32(*theta.shape), VMEM)],
        [vmem(matrix_shape, jnp.bfloat16), dma((matrix_shape[0],))],
    )(arrived.reshape(blocks * 12 * WINDOW, LANES), matrix, local)


def solution(mesh):
    placed = (
        P(None, None, ("gy", "gx"), None, "gz"),
        P("gy", "gz", "gx"),
        P("gy", "gz", "gx"),
        P(),
        P(),
        P(),
        P(),
    )
    return jax.shard_map(
        body,
        mesh=mesh,
        in_specs=placed,
        out_specs=(P("gy", "gz", "gx"), P("gy", "gz", "gx")),
        check_vma=False,
    )
```

```python
import functools
import math

import jax
import jax.numpy as jnp
import numpy as np
from jax import lax
from jax.experimental import pallas as pl
from jax.experimental.pallas import tpu as pltpu
from jax.sharding import PartitionSpec as P

first_coeffs = (0.8, -0.2, 4.0 / 105.0, -1.0 / 280.0)
second_coeffs = (1.6, -0.2, 8.0 / 315.0, -1.0 / 560.0)
center_coeff = -205.0 / 72.0
diffusivity = 0.15
time_step = 0.4
section_keep = -5.0 / 9.0
section_gain = 15.0 / 16.0

LANES = 128
LOW = 32
SEGMENT = 6
WINDOW = 8
VMEM_LIMIT = 16 * 1024 * 1024


def halves(values):
    high = values.astype(jnp.bfloat16)
    return high, (values - high.astype(jnp.float32)).astype(jnp.bfloat16)


def numpy_halves(values):
    values = values.astype(np.float32)
    high = values.astype(jnp.bfloat16)
    return high, (values - high.astype(np.float32)).astype(jnp.bfloat16)


def dot(a, b):
    return jnp.dot(a, b, preferred_element_type=jnp.float32)


@functools.cache
def tables():
    j = np.arange(LANES)
    h, g = np.meshgrid(np.arange(4), np.arange(16), indexing="ij")
    angle = 2 * math.pi * (((4 * g + h)[:, :, None] * j) % LANES) / LANES
    real_rows = np.concatenate([np.cos(angle), np.sin(angle)], -1)
    imag_rows = np.concatenate([-np.sin(angle), np.cos(angle)], -1)
    first = np.stack([real_rows, imag_rows], 1).reshape(LANES, 2 * LANES)
    first_high, first_low = numpy_halves(first)
    low = np.arange(LOW)
    twist = 2 * math.pi * (low[:, None] * j[None, :]) / (LOW * LANES)
    twiddle = np.stack([np.cos(twist), np.sin(twist)]).astype(np.float32)
    m = np.arange(LOW)[:, None, None] + np.arange(WINDOW)[:, None]
    last_angle = 2 * math.pi * ((m * low) % LOW) / LOW
    last = np.concatenate([np.cos(last_angle), -np.sin(last_angle)], -1)
    last_high, last_low = (t.astype(np.float32) for t in numpy_halves(last))
    last_all = np.concatenate([last_high, last_low, last_high], -1)
    return np.concatenate([first_high, first_high, first_low], 0), twiddle, last_all


def pack_kernel(spectrum_ref, theta_ref, out_ref, low_ref, high_ref, got, packed, sems):
    groups, dests, rows = 2, out_ref.shape[0], theta_ref.shape[0]
    count = dests // groups
    heads = [
        pltpu.make_async_copy(
            spectrum_ref.at[:, pl.ds(4 * count * group, 4 * count), :],
            got.at[:, pl.ds(4 * count * group, 4 * count), :],
            sems.at[group],
        )
        for group in range(groups)
    ]
    tails = [
        pltpu.make_async_copy(
            packed.at[pl.ds(count * group, count)],
            out_ref.at[pl.ds(count * group, count)],
            sems.at[groups + group],
        )
        for group in range(groups)
    ]
    sides = [
        pltpu.make_async_copy(theta_ref.at[pl.ds(0, 4)], low_ref, sems.at[2 * groups]),
        pltpu.make_async_copy(theta_ref.at[pl.ds(rows - 4, 4)], high_ref, sems.at[2 * groups + 1]),
    ]
    for copy in heads + sides:
        copy.start()
    for group in range(groups):
        heads[group].wait()
        for dest in range(count * group, count * (group + 1)):
            for part in range(6):
                packed[dest, 4 * part : 4 * part + 4, :] = got[part, 4 * dest : 4 * dest + 4, :]
        tails[group].start()
    for copy in tails + sides:
        copy.wait()


def edges_of(theta_ref):
    spot = lax.broadcasted_iota(jnp.int32, (8, LANES), 1)
    edges = jnp.zeros((8, LANES), jnp.float32)
    cells = theta_ref.shape[2]
    for z in range(4):
        tail = pltpu.roll(theta_ref[:, z, cells - LANES :], (8 * z + 4) % LANES, 1)
        head = pltpu.roll(theta_ref[:, z, :LANES], 8 * z + 4, 1)
        edges = jnp.where((spot >= 8 * z) & (spot < 8 * z + 4), tail, edges)
        edges = jnp.where((spot >= 8 * z + 4) & (spot < 8 * z + 8), head, edges)
    return edges


def setup_kernel(
    offset_hbm, theta_hbm, last_hbm, first_hbm, twiddle_hbm,
    left_ref, turn_ref, edges_ref, first_ref, twiddle_ref,
    offset, theta, last, sems,
):
    moves = ((offset_hbm, offset), (theta_hbm, theta), (last_hbm, last))
    moves += ((first_hbm, first_ref), (twiddle_hbm, twiddle_ref))
    copies = [
        pltpu.make_async_copy(source, target, sems.at[number])
        for number, (source, target) in enumerate(moves)
    ]
    for copy in copies:
        copy.start()
    for copy in copies:
        copy.wait()
    blocks = left_ref.shape[0] // WINDOW
    left = [last[offset[block] // LANES] for block in range(blocks)]
    left_ref[...] = jnp.concatenate(left, 0).astype(jnp.bfloat16)
    lane = lax.broadcasted_iota(jnp.int32, (1, LANES), 1)
    for block in range(blocks):
        turn_ref[block : block + 1, :] = jnp.where(lane < offset[block] % LANES, 1.0, 0.0)
    edges_ref[...] = edges_of(theta)


def matrix_kernel(
    offset_hbm, length_hbm, index_hbm, weight_hbm, after_ref,
    near_ref, far_hbm,
    offset, length, index_ref, weight_ref, far_ref, sems, out_sems,
):
    block = lax.axis_index("gx")
    cells = index_ref.shape[1]
    mine = pl.ds(pl.multiple_of(block * cells, LANES), cells)
    moves = ((offset_hbm, offset), (length_hbm, length))
    moves += ((index_hbm.at[:, mine], index_ref), (weight_hbm.at[:, mine], weight_ref))
    heads = [
        pltpu.make_async_copy(source, target, sems.at[number])
        for number, (source, target) in enumerate(moves)
    ]
    for copy in heads:
        copy.start()
    for copy in heads:
        copy.wait()
    start, live = offset[block], length[block]
    rows = lax.broadcasted_iota(jnp.int32, (8, LANES), 0)
    taps = index_ref.shape[0]
    copies = []
    half_pairs = near_ref.shape[0]
    for number in range(2 * half_pairs):
        pair = (number + half_pairs) % (2 * half_pairs)
        matrix, place = (near_ref, pair) if pair < half_pairs else (far_ref, pair - half_pairs)
        for side in range(2):
            lanes = slice((2 * pair + side) * LANES, (2 * pair + side + 1) * LANES)
            index = index_ref[:, lanes]
            weight = jnp.where(index < live, weight_ref[:, lanes], 0.0)
            inner = lax.rem(index + start, LANES)
            spots = [jnp.broadcast_to(inner[t : t + 1], (8, LANES)) for t in range(taps)]
            parts = []
            for m in range(SEGMENT):
                part = jnp.where(index // LANES == m, weight, 0.0)
                parts.append([jnp.broadcast_to(part[t : t + 1], (8, LANES)) for t in range(taps)])

            def step(number, carry, side=side, matrix=matrix, place=place, spots=spots, parts=parts):
                near = [rows + 16 * number, rows + (16 * number + 8)]
                hits = [[near[half] == spots[t] for t in range(taps)] for half in range(2)]
                for m in range(SEGMENT):
                    total = []
                    for half in range(2):
                        terms = [jnp.where(hits[half][t], parts[m][t], 0.0) for t in range(taps)]
                        while len(terms) > 1:
                            terms = [a + b for a, b in zip(terms[::2], terms[1::2], strict=True)]
                        total.append(terms[0])
                    high, low = halves(jnp.concatenate(total, 0))
                    at = pl.ds(pl.multiple_of(LANES * m + 16 * number, 16), 16)
                    matrix[place, 0, at, side * LANES : (side + 1) * LANES] = high
                    matrix[place, 1, at, side * LANES : (side + 1) * LANES] = low
                return carry

            lax.fori_loop(0, LANES // 16, step, 0)
        if pair >= half_pairs:
            copy = pltpu.make_async_copy(
                far_ref.at[place], far_hbm.at[place], out_sems.at[place]
            )
            copies.append(copy)
            copy.start()
    for copy in copies:
        copy.wait()


def transform_kernel(
    got_ref, first_ref, twiddle_ref, left_ref, turn_ref, edges_ref, *after_and_out
):
    out_ref = after_and_out[-1]
    lane = lax.broadcasted_iota(jnp.int32, (LOW, LANES), 1) // LOW
    pieces = []
    for comp in range(3):
        rows = [
            got_ref[pl.ds(comp * 8 + part * 4 + z, 16, stride=24), :]
            for z in range(4)
            for part in range(2)
        ]
        turned = jnp.concatenate(rows, 0).T
        for z in range(4):
            piece = jnp.zeros((LOW, LANES), jnp.float32)
            for h in range(4):
                moved = turned[LOW * h : LOW * (h + 1), :]
                if h != z:
                    moved = pltpu.roll(moved, (LOW * (h - z)) % LANES, 1)
                piece = jnp.where(lane == h, moved, piece)
            pieces.append(piece)
    high, low = halves(jnp.concatenate(pieces, 0))
    done = dot(jnp.concatenate([high, low], 1), first_ref[: 2 * LANES, :]) + dot(
        high, first_ref[2 * LANES :, :]
    )
    cosine, sine = twiddle_ref[0], twiddle_ref[1]
    right = []
    for line in range(12):
        real = done[LOW * line : LOW * (line + 1), :LANES]
        imag = done[LOW * line : LOW * (line + 1), LANES:]
        high, low = halves(
            jnp.concatenate([real * cosine - imag * sine, real * sine + imag * cosine], 0)
        )
        right.append(jnp.concatenate([high, high, low], 0))
    lines = dot(left_ref[...], jnp.concatenate(right, 1))
    for block in range(out_ref.shape[0]):
        turned = jnp.broadcast_to(turn_ref[block : block + 1, :], (WINDOW, LANES)) > 0.5
        for line in range(12):
            cells = lines[WINDOW * block : WINDOW * (block + 1), line * LANES : (line + 1) * LANES]
            out_ref[block, line] = jnp.where(turned, pltpu.roll(cells, WINDOW - 1, 0), cells)
    for block in range(out_ref.shape[0]):
        for y in range(8):
            out_ref[block, y, WINDOW - 1 :, :] = edges_ref[y : y + 1]


def stencil_kernel(
    z_low_ref, z_high_ref, y_low_ref, y_high_ref, theta_ref, sum_ref, after_ref,
    local_hbm,
    local_ref, sems,
):
    cells = theta_ref.shape[2]
    lane = lax.broadcasted_iota(jnp.int32, (8, cells), 1)
    planes = [ref[:, z, :] for ref in (z_low_ref, theta_ref, z_high_ref) for z in range(4)]
    for z in range(4):
        here = planes[4 + z]
        column = jnp.concatenate([y_low_ref[:, z, :], here, y_high_ref[:, z, :]], 0)
        grad_x = jnp.zeros_like(here)
        grad_y = jnp.zeros_like(here)
        grad_z = jnp.zeros_like(here)
        laplace = 3.0 * center_coeff * here
        for reach in range(1, 5):
            first = -time_step * first_coeffs[reach - 1]
            ahead_x = jnp.where(lane < cells - reach, pltpu.roll(here, cells - reach, 1), 0.0)
            behind_x = jnp.where(lane >= reach, pltpu.roll(here, reach, 1), 0.0)
            ahead_y = column[4 + reach : 12 + reach]
            behind_y = column[4 - reach : 12 - reach]
            ahead_z = planes[4 + z + reach]
            behind_z = planes[4 + z - reach]
            grad_x = grad_x + first * (ahead_x - behind_x)
            grad_y = grad_y + first * (ahead_y - behind_y)
            grad_z = grad_z + first * (ahead_z - behind_z)
            laplace = laplace + second_coeffs[reach - 1] * (
                (ahead_x + behind_x) + (ahead_y + behind_y) + (ahead_z + behind_z)
            )
        local_ref[0, z] = grad_x
        local_ref[1, z] = grad_y
        local_ref[2, z] = grad_z
        local_ref[3, z] = section_keep * sum_ref[:, z, :] + (time_step * diffusivity) * laplace
        local_ref[4, z] = here
    copy = pltpu.make_async_copy(local_ref, local_hbm, sems.at[0])
    copy.start()
    copy.wait()


def combine_kernel(
    got_ref, near_ref, far_hbm, local_hbm, theta_ref, section_ref, far_ref, local_ref, sems
):
    half_pairs = near_ref.shape[0]
    copies = [
        pltpu.make_async_copy(far_hbm.at[pair], far_ref.at[pair], sems.at[pair])
        for pair in range(half_pairs)
    ]
    copies.append(pltpu.make_async_copy(local_hbm, local_ref, sems.at[half_pairs]))
    for copy in copies[::-1]:
        copy.start()
    block = lax.axis_index("gx")
    blocks = got_ref.shape[0] // (12 * WINDOW)
    cells = local_ref.shape[3]
    rows = [
        jnp.concatenate(
            [
                got_ref[pl.ds(WINDOW * line + m, blocks, stride=12 * WINDOW), :]
                for line in range(12)
            ],
            0,
        )
        for m in range(SEGMENT)
    ]
    high, low = halves(jnp.concatenate(rows, 1))
    both = jnp.concatenate([high, low], 0)
    count = high.shape[0]

    def halo_of(source):
        return got_ref[pl.ds(source * 12 * WINDOW + WINDOW - 1, 8, stride=WINDOW), :]

    before = halo_of(lax.rem(block + blocks - 1, blocks))
    after = halo_of(lax.rem(block + 1, blocks))
    lane = lax.broadcasted_iota(jnp.int32, (8, LANES), 1)
    width = 2 * LANES
    for tile in range(cells // width):
        lanes = slice(tile * width, (tile + 1) * width)
        matrix, pair = near_ref, tile
        if tile >= half_pairs:
            matrix, pair = far_ref, tile - half_pairs
            copies[pair].wait()
        twice = dot(both, matrix[pair, 0])
        carried = twice[:count] + twice[count:] + dot(high, matrix[pair, 1])
        if tile == 0:
            copies[half_pairs].wait()
        for z in range(4):
            grad_x = local_ref[0, z, :, lanes]
            base = local_ref[3, z, :, lanes]
            if tile == 0 or (tile + 1) * width == cells:
                more_grad = jnp.zeros((8, LANES), jnp.float32)
                more_base = jnp.zeros((8, LANES), jnp.float32)
                for reach in range(1, 5):
                    if tile == 0:
                        moved = pltpu.roll(before, (LANES - 4 - 8 * z + reach) % LANES, 1)
                        halo = jnp.where(lane < reach, moved, 0.0)
                        sign = 1.0
                    else:
                        moved = pltpu.roll(after, (LANES - 4 - 8 * z - reach) % LANES, 1)
                        halo = jnp.where(lane >= LANES - reach, moved, 0.0)
                        sign = -1.0
                    more_grad = more_grad + (sign * time_step * first_coeffs[reach - 1]) * halo
                    more_base = (
                        more_base + (time_step * diffusivity * second_coeffs[reach - 1]) * halo
                    )
                none = jnp.zeros((8, LANES), jnp.float32)
                order = (lambda v: [v, none]) if tile == 0 else (lambda v: [none, v])
                grad_x = grad_x + jnp.concatenate(order(more_grad), 1)
                base = base + jnp.concatenate(order(more_base), 1)
            section = (
                base
                + carried[8 * z : 8 * z + 8] * grad_x
                + carried[32 + 8 * z : 40 + 8 * z] * local_ref[1, z, :, lanes]
                + carried[64 + 8 * z : 72 + 8 * z] * local_ref[2, z, :, lanes]
            )
            section_ref[:, z, lanes] = section
            theta_ref[:, z, lanes] = local_ref[4, z, :, lanes] + section_gain * section


def f32(*shape):
    return jax.ShapeDtypeStruct(shape, jnp.float32)


def bf16(*shape):
    return jax.ShapeDtypeStruct(shape, jnp.bfloat16)


VMEM = pl.BlockSpec(memory_space=pltpu.VMEM)
HBM = pl.BlockSpec(memory_space=pltpu.HBM)
ANY = pl.BlockSpec(memory_space=pl.ANY)


def in_hbm(array):
    return pltpu.with_memory_space_constraint(array, pltpu.HBM)


def run(kernel, name, in_specs, outs, scratch=()):
    return pl.pallas_call(
        kernel,
        out_shape=tuple(shape for shape, _ in outs),
        in_specs=in_specs,
        out_specs=tuple(spec for _, spec in outs),
        scratch_shapes=scratch,
        compiler_params=pltpu.CompilerParams(vmem_limit_bytes=VMEM_LIMIT),
        cost_estimate=pl.CostEstimate(flops=4 * 10**9, bytes_accessed=4 * 10**6, transcendentals=0),
        name=name,
    )


def neighbours(edge_low, edge_high, axis):
    count = lax.axis_size(axis)
    up = [(i, (i + 1) % count) for i in range(count)]
    return lax.ppermute(edge_high, axis, up), lax.ppermute(edge_low, axis, [(b, a) for a, b in up])


def body(spectrum, theta, section_sum, seg_offset, seg_length, stencil_index, stencil_weight):
    blocks, depth = lax.axis_size("gx"), lax.axis_size("gz")
    rows_count, layers, cells = theta.shape
    taps = stencil_index.shape[0]
    first, twiddle, last = (jnp.asarray(t) for t in tables())
    vmem, smem, dma = pltpu.VMEM, pltpu.SMEM, pltpu.SemaphoreType.DMA

    edge = f32(4, layers, cells)
    packed, y_first, y_last = run(
        pack_kernel,
        "pack",
        [HBM, HBM],
        [(f32(depth, 24, LANES), HBM), (edge, HBM), (edge, HBM)],
        [vmem((6, 4 * depth, LANES), jnp.float32), vmem((depth, 24, LANES), jnp.float32), dma((6,))],
    )(in_hbm(spectrum.reshape(6, 4 * depth, LANES)), in_hbm(theta))
    columns = lax.all_to_all(packed, "gz", split_axis=0, concat_axis=0, tiled=True)
    z_low, z_high = neighbours(theta, theta, "gz")
    y_low, y_high = neighbours(y_first, y_last, "gy")
    left, turn, edges, first, twiddle = run(
        setup_kernel,
        "setup",
        [HBM] * 5,
        [
            (bf16(blocks * WINDOW, last.shape[2]), VMEM),
            (f32(blocks, LANES), VMEM),
            (f32(8, LANES), VMEM),
            (bf16(*first.shape), VMEM),
            (f32(*twiddle.shape), VMEM),
        ],
        [smem((blocks,), jnp.int32), vmem(theta.shape, jnp.float32), vmem(last.shape, jnp.float32)]
        + [dma((5,))],
    )(seg_offset, theta, last, first, twiddle)
    (pieces,) = run(
        transform_kernel,
        "transform",
        [VMEM] * 6 + [ANY] * 2,
        [(f32(blocks, 12, WINDOW, LANES), VMEM)],
    )(columns.reshape(depth * 24, LANES), first, twiddle, left, turn, edges, z_low, z_high)
    arrived = lax.all_to_all(pieces, "gx", split_axis=0, concat_axis=0, tiled=True)
    half_pairs = cells // (4 * LANES)
    half = (half_pairs, 2, SEGMENT * LANES, 2 * LANES)
    near, far = run(
        matrix_kernel,
        "matrix",
        [HBM] * 4 + [ANY],
        [(bf16(*half), VMEM), (pltpu.HBM(half, jnp.bfloat16), HBM)],
        [smem((blocks,), jnp.int32), smem((blocks,), jnp.int32)]
        + [vmem((taps, cells), jnp.int32), vmem((taps, cells), jnp.float32)]
        + [vmem(half, jnp.bfloat16), dma((4,)), dma((half_pairs,))],
    )(seg_offset, seg_length, stencil_index, stencil_weight, pieces)
    local_shape = (5, layers, rows_count, cells)
    (local,) = run(
        stencil_kernel,
        "stencil",
        [VMEM] * 6 + [ANY],
        [(pltpu.HBM(local_shape, jnp.float32), HBM)],
        [vmem(local_shape, jnp.float32), dma((1,))],
    )(z_low, z_high, y_low, y_high, theta, section_sum, pieces)
    return run(
        combine_kernel,
        "combine",
        [VMEM, VMEM, HBM, HBM],
        [(f32(*theta.shape), VMEM), (f32(*theta.shape), VMEM)],
        [vmem(half, jnp.bfloat16), vmem(local_shape, jnp.float32), dma((half_pairs + 1,))],
    )(arrived.reshape(blocks * 12 * WINDOW, LANES), near, in_hbm(far), in_hbm(local))


def solution(mesh):
    placed = (
        P(None, None, ("gy", "gx"), None, "gz"),
        P("gy", "gz", "gx"),
        P("gy", "gz", "gx"),
        P(),
        P(),
        P(),
        P(),
    )
    return jax.shard_map(
        body,
        mesh=mesh,
        in_specs=placed,
        out_specs=(P("gy", "gz", "gx"), P("gy", "gz", "gx")),
        check_vma=False,
    )
```

```python
import functools
import math

import jax
import jax.numpy as jnp
import numpy as np
from jax import lax
from jax.experimental import pallas as pl
from jax.experimental.pallas import tpu as pltpu
from jax.sharding import PartitionSpec as P

first_coeffs = (0.8, -0.2, 4.0 / 105.0, -1.0 / 280.0)
second_coeffs = (1.6, -0.2, 8.0 / 315.0, -1.0 / 560.0)
center_coeff = -205.0 / 72.0
diffusivity = 0.15
time_step = 0.4
section_keep = -5.0 / 9.0
section_gain = 15.0 / 16.0

LANES = 128
LOW = 32
SEGMENT = 6
PAIRS = 4
NEAR = 2
WINDOW = 8
VMEM_LIMIT = 16 * 1024 * 1024


def halves(values):
    high = values.astype(jnp.bfloat16)
    return high, (values - high.astype(jnp.float32)).astype(jnp.bfloat16)


def numpy_halves(values):
    values = values.astype(np.float32)
    high = values.astype(jnp.bfloat16)
    return high, (values - high.astype(np.float32)).astype(jnp.bfloat16)


def dot(a, b):
    return jnp.dot(a, b, preferred_element_type=jnp.float32)


@functools.cache
def tables():
    j = np.arange(LANES)
    h, g = np.meshgrid(np.arange(4), np.arange(16), indexing="ij")
    angle = 2 * math.pi * (((4 * g + h)[:, :, None] * j) % LANES) / LANES
    real_rows = np.concatenate([np.cos(angle), np.sin(angle)], -1)
    imag_rows = np.concatenate([-np.sin(angle), np.cos(angle)], -1)
    first = np.stack([real_rows, imag_rows], 1).reshape(LANES, 2 * LANES)
    first_high, first_low = numpy_halves(first)
    low = np.arange(LOW)
    twist = 2 * math.pi * (low[:, None] * j[None, :]) / (LOW * LANES)
    twiddle = np.stack([np.cos(twist), np.sin(twist)]).astype(np.float32)
    m = np.arange(LOW)[:, None, None] + np.arange(WINDOW)[:, None]
    last_angle = 2 * math.pi * ((m * low) % LOW) / LOW
    last = np.concatenate([np.cos(last_angle), -np.sin(last_angle)], -1)
    last_high, last_low = (t.astype(np.float32) for t in numpy_halves(last))
    last_all = np.concatenate([last_high, last_low, last_high], -1)
    return np.concatenate([first_high, first_high, first_low], 0), twiddle, last_all


def pack_kernel(spectrum_ref, theta_ref, out_ref, low_ref, high_ref, got, packed, sems):
    groups, dests, rows = 4, out_ref.shape[0], theta_ref.shape[0]
    count = dests // groups
    heads = [
        pltpu.make_async_copy(
            spectrum_ref.at[:, pl.ds(4 * count * group, 4 * count), :],
            got.at[:, pl.ds(4 * count * group, 4 * count), :],
            sems.at[group],
        )
        for group in range(groups)
    ]
    tails = [
        pltpu.make_async_copy(
            packed.at[pl.ds(count * group, count)],
            out_ref.at[pl.ds(count * group, count)],
            sems.at[groups + group],
        )
        for group in range(groups)
    ]
    sides = [
        pltpu.make_async_copy(theta_ref.at[pl.ds(0, 4)], low_ref, sems.at[2 * groups]),
        pltpu.make_async_copy(theta_ref.at[pl.ds(rows - 4, 4)], high_ref, sems.at[2 * groups + 1]),
    ]
    for copy in heads + sides:
        copy.start()
    for group in range(groups):
        heads[group].wait()
        for dest in range(count * group, count * (group + 1)):
            for part in range(6):
                packed[dest, 4 * part : 4 * part + 4, :] = got[part, 4 * dest : 4 * dest + 4, :]
        tails[group].start()
    for copy in tails + sides:
        copy.wait()


def edges_of(theta_ref):
    spot = lax.broadcasted_iota(jnp.int32, (8, LANES), 1)
    edges = jnp.zeros((8, LANES), jnp.float32)
    cells = theta_ref.shape[2]
    for z in range(4):
        tail = pltpu.roll(theta_ref[:, z, cells - LANES :], (8 * z + 4) % LANES, 1)
        head = pltpu.roll(theta_ref[:, z, :LANES], 8 * z + 4, 1)
        edges = jnp.where((spot >= 8 * z) & (spot < 8 * z + 4), tail, edges)
        edges = jnp.where((spot >= 8 * z + 4) & (spot < 8 * z + 8), head, edges)
    return edges


def setup_kernel(
    offset_hbm, theta_hbm, last_hbm, first_hbm, twiddle_hbm,
    left_ref, turn_ref, edges_ref, first_ref, twiddle_ref, theta,
    offset, last, sems,
):
    moves = ((offset_hbm, offset), (theta_hbm, theta), (last_hbm, last))
    moves += ((first_hbm, first_ref), (twiddle_hbm, twiddle_ref))
    copies = [
        pltpu.make_async_copy(source, target, sems.at[number])
        for number, (source, target) in enumerate(moves)
    ]
    for copy in copies:
        copy.start()
    for copy in copies:
        copy.wait()
    blocks = left_ref.shape[0] // WINDOW
    left = [last[offset[block] // LANES] for block in range(blocks)]
    left_ref[...] = jnp.concatenate(left, 0).astype(jnp.bfloat16)
    lane = lax.broadcasted_iota(jnp.int32, (1, LANES), 1)
    for block in range(blocks):
        turn_ref[block : block + 1, :] = jnp.where(lane < offset[block] % LANES, 1.0, 0.0)
    edges_ref[...] = edges_of(theta)


def matrix_kernel(
    near, offset_hbm, length_hbm, index_ref, weight_ref, after_ref, *outs_and_scratch
):
    count = PAIRS
    refs, far_hbms = outs_and_scratch[:near], outs_and_scratch[near:count]
    offset, length = outs_and_scratch[count : count + 2]
    refs = refs + outs_and_scratch[count + 2 : -2]
    sems, out_sems = outs_and_scratch[-2:]
    block = lax.axis_index("gx")
    cells = index_ref.shape[1] // lax.axis_size("gx")
    first_cell = block * cells
    heads = [
        pltpu.make_async_copy(source, target, sems.at[number])
        for number, (source, target) in enumerate(((offset_hbm, offset), (length_hbm, length)))
    ]
    for copy in heads:
        copy.start()
    for copy in heads:
        copy.wait()
    start, live = offset[block], length[block]
    rows = lax.broadcasted_iota(jnp.int32, (8, LANES), 0)
    taps = index_ref.shape[0]
    copies = []
    for number in range(PAIRS):
        pair = (number + near) % PAIRS
        matrix = refs[pair]
        for side in range(2):
            lanes = pl.ds(pl.multiple_of(first_cell + (2 * pair + side) * LANES, LANES), LANES)
            index = index_ref[:, lanes]
            weight = jnp.where(index < live, weight_ref[:, lanes], 0.0)
            inner = lax.rem(index + start, LANES)
            spots = [jnp.broadcast_to(inner[t : t + 1], (8, LANES)) for t in range(taps)]
            parts = []
            for m in range(SEGMENT):
                part = jnp.where(index // LANES == m, weight, 0.0)
                parts.append([jnp.broadcast_to(part[t : t + 1], (8, LANES)) for t in range(taps)])

            def step(number, carry, side=side, matrix=matrix, spots=spots, parts=parts):
                sums = []
                for half in range(2):
                    near = rows + (16 * number + 8 * half)
                    hits = [near == spots[t] for t in range(taps)]
                    for m in range(SEGMENT):
                        total = jnp.where(hits[0], parts[m][0], 0.0)
                        for t in range(1, taps):
                            total = jnp.where(hits[t], total + parts[m][t], total)
                        sums.append(total)
                for m in range(SEGMENT):
                    high, low = halves(jnp.concatenate([sums[m], sums[SEGMENT + m]], 0))
                    at = pl.ds(pl.multiple_of(LANES * m + 16 * number, 16), 16)
                    matrix[0, at, side * LANES : (side + 1) * LANES] = high
                    matrix[1, at, side * LANES : (side + 1) * LANES] = low
                return carry

            lax.fori_loop(0, LANES // 16, step, 0)
        if pair >= near:
            copies.append(
                pltpu.make_async_copy(matrix, far_hbms[pair - near], out_sems.at[pair - near])
            )
            copies[-1].start()
    for copy in copies:
        copy.wait()


def transform_kernel(
    got_ref, first_ref, twiddle_ref, left_ref, turn_ref, edges_ref, *after_and_out
):
    out_ref = after_and_out[-1]
    lane = lax.broadcasted_iota(jnp.int32, (LOW, LANES), 1) // LOW
    pieces = []
    for comp in range(3):
        rows = [
            got_ref[pl.ds(comp * 8 + part * 4 + z, 16, stride=24), :]
            for z in range(4)
            for part in range(2)
        ]
        turned = jnp.concatenate(rows, 0).T
        for z in range(4):
            piece = jnp.zeros((LOW, LANES), jnp.float32)
            for h in range(4):
                moved = turned[LOW * h : LOW * (h + 1), :]
                if h != z:
                    moved = pltpu.roll(moved, (LOW * (h - z)) % LANES, 1)
                piece = jnp.where(lane == h, moved, piece)
            pieces.append(piece)
    high, low = halves(jnp.concatenate(pieces, 0))
    done = dot(jnp.concatenate([high, low], 1), first_ref[: 2 * LANES, :]) + dot(
        high, first_ref[2 * LANES :, :]
    )
    cosine, sine = twiddle_ref[0], twiddle_ref[1]
    right = []
    for line in range(12):
        real = done[LOW * line : LOW * (line + 1), :LANES]
        imag = done[LOW * line : LOW * (line + 1), LANES:]
        high, low = halves(
            jnp.concatenate([real * cosine - imag * sine, real * sine + imag * cosine], 0)
        )
        right.append(jnp.concatenate([high, high, low], 0))
    lines = dot(left_ref[...], jnp.concatenate(right, 1))
    for block in range(out_ref.shape[0]):
        turned = jnp.broadcast_to(turn_ref[block : block + 1, :], (WINDOW, LANES)) > 0.5
        for line in range(12):
            cells = lines[WINDOW * block : WINDOW * (block + 1), line * LANES : (line + 1) * LANES]
            out_ref[block, line] = jnp.where(turned, pltpu.roll(cells, WINDOW - 1, 0), cells)
    for block in range(out_ref.shape[0]):
        for y in range(8):
            out_ref[block, y, WINDOW - 1 :, :] = edges_ref[y : y + 1]


def stencil_kernel(
    z_low_ref, z_high_ref, y_low_ref, y_high_ref, theta_ref, sum_ref, after_ref,
    local_hbm,
    local_ref, sems,
):
    cells = theta_ref.shape[2]
    lane = lax.broadcasted_iota(jnp.int32, (8, cells), 1)
    planes = [ref[:, z, :] for ref in (z_low_ref, theta_ref, z_high_ref) for z in range(4)]
    for z in range(4):
        here = planes[4 + z]
        column = jnp.concatenate([y_low_ref[:, z, :], here, y_high_ref[:, z, :]], 0)
        grad_x = jnp.zeros_like(here)
        grad_y = jnp.zeros_like(here)
        grad_z = jnp.zeros_like(here)
        laplace = 3.0 * center_coeff * here
        for reach in range(1, 5):
            first = -time_step * first_coeffs[reach - 1]
            ahead_x = jnp.where(lane < cells - reach, pltpu.roll(here, cells - reach, 1), 0.0)
            behind_x = jnp.where(lane >= reach, pltpu.roll(here, reach, 1), 0.0)
            ahead_y = column[4 + reach : 12 + reach]
            behind_y = column[4 - reach : 12 - reach]
            ahead_z = planes[4 + z + reach]
            behind_z = planes[4 + z - reach]
            grad_x = grad_x + first * (ahead_x - behind_x)
            grad_y = grad_y + first * (ahead_y - behind_y)
            grad_z = grad_z + first * (ahead_z - behind_z)
            laplace = laplace + second_coeffs[reach - 1] * (
                (ahead_x + behind_x) + (ahead_y + behind_y) + (ahead_z + behind_z)
            )
        local_ref[0, z] = grad_x
        local_ref[1, z] = grad_y
        local_ref[2, z] = grad_z
        local_ref[3, z] = section_keep * sum_ref[:, z, :] + (time_step * diffusivity) * laplace
        local_ref[4, z] = here
    copy = pltpu.make_async_copy(local_ref, local_hbm, sems.at[0])
    copy.start()
    copy.wait()


def combine_kernel(near, got_ref, local_hbm, *refs):
    matrices, far_hbms = refs[:near] + refs[PAIRS + 2 : -2], refs[near:PAIRS]
    theta_ref, section_ref = refs[PAIRS : PAIRS + 2]
    local_ref, sems = refs[-2:]
    moves = list(zip(far_hbms, matrices[near:], strict=True)) + [(local_hbm, local_ref)]
    copies = [
        pltpu.make_async_copy(source, target, sems.at[number])
        for number, (source, target) in enumerate(moves)
    ]
    for copy in copies:
        copy.start()
    block = lax.axis_index("gx")
    blocks = got_ref.shape[0] // (12 * WINDOW)
    cells = local_ref.shape[3]
    rows = [
        jnp.concatenate(
            [
                got_ref[pl.ds(WINDOW * line + m, blocks, stride=12 * WINDOW), :]
                for line in range(12)
            ],
            0,
        )
        for m in range(SEGMENT)
    ]
    high, low = halves(jnp.concatenate(rows, 1))
    both = jnp.concatenate([high, low], 0)
    count = high.shape[0]

    def halo_of(source):
        return got_ref[pl.ds(source * 12 * WINDOW + WINDOW - 1, 8, stride=WINDOW), :]

    before = halo_of(lax.rem(block + blocks - 1, blocks))
    after = halo_of(lax.rem(block + 1, blocks))
    lane = lax.broadcasted_iota(jnp.int32, (8, LANES), 1)
    width = 2 * LANES
    carried_of = []
    for tile in range(cells // width):
        if tile >= near:
            copies[tile - near].wait()
        twice = dot(both, matrices[tile][0])
        carried_of.append(twice[:count] + twice[count:] + dot(high, matrices[tile][1]))
    copies[-1].wait()
    for tile in range(cells // width):
        lanes = slice(tile * width, (tile + 1) * width)
        carried = carried_of[tile]
        for z in range(4):
            grad_x = local_ref[0, z, :, lanes]
            base = local_ref[3, z, :, lanes]
            if tile == 0 or (tile + 1) * width == cells:
                more_grad = jnp.zeros((8, LANES), jnp.float32)
                more_base = jnp.zeros((8, LANES), jnp.float32)
                for reach in range(1, 5):
                    if tile == 0:
                        moved = pltpu.roll(before, (LANES - 4 - 8 * z + reach) % LANES, 1)
                        halo = jnp.where(lane < reach, moved, 0.0)
                        sign = 1.0
                    else:
                        moved = pltpu.roll(after, (LANES - 4 - 8 * z - reach) % LANES, 1)
                        halo = jnp.where(lane >= LANES - reach, moved, 0.0)
                        sign = -1.0
                    more_grad = more_grad + (sign * time_step * first_coeffs[reach - 1]) * halo
                    more_base = (
                        more_base + (time_step * diffusivity * second_coeffs[reach - 1]) * halo
                    )
                none = jnp.zeros((8, LANES), jnp.float32)
                order = (lambda v: [v, none]) if tile == 0 else (lambda v: [none, v])
                grad_x = grad_x + jnp.concatenate(order(more_grad), 1)
                base = base + jnp.concatenate(order(more_base), 1)
            section = (
                base
                + carried[8 * z : 8 * z + 8] * grad_x
                + carried[32 + 8 * z : 40 + 8 * z] * local_ref[1, z, :, lanes]
                + carried[64 + 8 * z : 72 + 8 * z] * local_ref[2, z, :, lanes]
            )
            section_ref[:, z, lanes] = section
            theta_ref[:, z, lanes] = local_ref[4, z, :, lanes] + section_gain * section


def f32(*shape):
    return jax.ShapeDtypeStruct(shape, jnp.float32)


def bf16(*shape):
    return jax.ShapeDtypeStruct(shape, jnp.bfloat16)


VMEM = pl.BlockSpec(memory_space=pltpu.VMEM)
HBM = pl.BlockSpec(memory_space=pltpu.HBM)
ANY = pl.BlockSpec(memory_space=pl.ANY)


def in_hbm(array):
    return pltpu.with_memory_space_constraint(array, pltpu.HBM)


def run(kernel, name, in_specs, outs, scratch=()):
    return pl.pallas_call(
        kernel,
        out_shape=tuple(shape for shape, _ in outs),
        in_specs=in_specs,
        out_specs=tuple(spec for _, spec in outs),
        scratch_shapes=scratch,
        compiler_params=pltpu.CompilerParams(vmem_limit_bytes=VMEM_LIMIT),
        cost_estimate=pl.CostEstimate(flops=4 * 10**9, bytes_accessed=4 * 10**6, transcendentals=0),
        name=name,
    )


def neighbours(edge_low, edge_high, axis):
    count = lax.axis_size(axis)
    up = [(i, (i + 1) % count) for i in range(count)]
    return lax.ppermute(edge_high, axis, up), lax.ppermute(edge_low, axis, [(b, a) for a, b in up])


def body(spectrum, theta, section_sum, seg_offset, seg_length, stencil_index, stencil_weight):
    blocks, depth = lax.axis_size("gx"), lax.axis_size("gz")
    rows_count, layers, cells = theta.shape
    first, twiddle, last = (jnp.asarray(t) for t in tables())
    vmem, smem, dma = pltpu.VMEM, pltpu.SMEM, pltpu.SemaphoreType.DMA

    edge = f32(4, layers, cells)
    packed, y_first, y_last = run(
        pack_kernel,
        "pack",
        [HBM, HBM],
        [(f32(depth, 24, LANES), HBM), (edge, HBM), (edge, HBM)],
        [vmem((6, 4 * depth, LANES), jnp.float32), vmem((depth, 24, LANES), jnp.float32), dma((10,))],
    )(in_hbm(spectrum.reshape(6, 4 * depth, LANES)), in_hbm(theta))
    columns = lax.all_to_all(packed, "gz", split_axis=0, concat_axis=0, tiled=True)
    y_low, y_high = neighbours(y_first, y_last, "gy")
    left, turn, edges, first, twiddle, copied = run(
        setup_kernel,
        "setup",
        [HBM] * 5,
        [
            (bf16(blocks * WINDOW, last.shape[2]), VMEM),
            (f32(blocks, LANES), VMEM),
            (f32(8, LANES), VMEM),
            (bf16(*first.shape), VMEM),
            (f32(*twiddle.shape), VMEM),
            (f32(*theta.shape), VMEM),
        ],
        [smem((blocks,), jnp.int32), vmem(last.shape, jnp.float32)]
        + [dma((5,))],
    )(seg_offset, theta, last, first, twiddle)
    z_low, z_high = neighbours(copied, copied, "gz")
    (pieces,) = run(
        transform_kernel,
        "transform",
        [VMEM] * 6,
        [(f32(blocks, 12, WINDOW, LANES), VMEM)],
    )(columns.reshape(depth * 24, LANES), first, twiddle, left, turn, edges)
    arrived = lax.all_to_all(pieces, "gx", split_axis=0, concat_axis=0, tiled=True)
    part = (2, SEGMENT * LANES, cells // PAIRS)
    far_parts = [vmem(part, jnp.bfloat16)] * (PAIRS - NEAR)
    matrices = run(
        functools.partial(matrix_kernel, NEAR),
        "matrix",
        [HBM, HBM, VMEM, VMEM, ANY],
        [(bf16(*part), VMEM)] * NEAR + [(pltpu.HBM(part, jnp.bfloat16), HBM)] * (PAIRS - NEAR),
        [smem((blocks,), jnp.int32), smem((blocks,), jnp.int32)]
        + far_parts
        + [dma((2,)), dma((PAIRS,))],
    )(seg_offset, seg_length, stencil_index, stencil_weight, pieces)
    matrices = matrices[:NEAR] + tuple(in_hbm(far) for far in matrices[NEAR:])
    local_shape = (5, layers, rows_count, cells)
    (local,) = run(
        stencil_kernel,
        "stencil",
        [VMEM] * 6 + [ANY],
        [(pltpu.HBM(local_shape, jnp.float32), HBM)],
        [vmem(local_shape, jnp.float32), dma((1,))],
    )(z_low, z_high, y_low, y_high, theta, section_sum, pieces)
    return run(
        functools.partial(combine_kernel, NEAR),
        "combine",
        [VMEM, HBM] + [VMEM] * NEAR + [HBM] * (PAIRS - NEAR),
        [(f32(*theta.shape), VMEM), (f32(*theta.shape), VMEM)],
        far_parts + [vmem(local_shape, jnp.float32), dma((PAIRS + 1,))],
    )(arrived.reshape(blocks * 12 * WINDOW, LANES), in_hbm(local), *matrices)


def solution(mesh):
    placed = (
        P(None, None, ("gy", "gx"), None, "gz"),
        P("gy", "gz", "gx"),
        P("gy", "gz", "gx"),
        P(),
        P(),
        P(),
        P(),
    )
    return jax.shard_map(
        body,
        mesh=mesh,
        in_specs=placed,
        out_specs=(P("gy", "gz", "gx"), P("gy", "gz", "gx")),
        check_vma=False,
    )
```

```python
import functools
import math

import jax
import jax.numpy as jnp
import numpy as np
from jax import lax
from jax.experimental import pallas as pl
from jax.experimental.pallas import tpu as pltpu
from jax.sharding import PartitionSpec as P

first_coeffs = (0.8, -0.2, 4.0 / 105.0, -1.0 / 280.0)
second_coeffs = (1.6, -0.2, 8.0 / 315.0, -1.0 / 560.0)
center_coeff = -205.0 / 72.0
diffusivity = 0.15
time_step = 0.4
section_keep = -5.0 / 9.0
section_gain = 15.0 / 16.0

LANES = 128
LOW = 32
SEGMENT = 6
PAIRS = 4
NEAR = 2
WINDOW = 8
VMEM_LIMIT = 16 * 1024 * 1024


def halves(values):
    high = values.astype(jnp.bfloat16)
    return high, (values - high.astype(jnp.float32)).astype(jnp.bfloat16)


def numpy_halves(values):
    values = values.astype(np.float32)
    high = values.astype(jnp.bfloat16)
    return high, (values - high.astype(np.float32)).astype(jnp.bfloat16)


def dot(a, b):
    return jnp.dot(a, b, preferred_element_type=jnp.float32)


@functools.cache
def tables():
    j = np.arange(LANES)
    h, g = np.meshgrid(np.arange(4), np.arange(16), indexing="ij")
    angle = 2 * math.pi * (((4 * g + h)[:, :, None] * j) % LANES) / LANES
    real_rows = np.concatenate([np.cos(angle), np.sin(angle)], -1)
    imag_rows = np.concatenate([-np.sin(angle), np.cos(angle)], -1)
    first = np.stack([real_rows, imag_rows], 1).reshape(LANES, 2 * LANES)
    first_high, first_low = numpy_halves(first)
    low = np.arange(LOW)
    twist = 2 * math.pi * (low[:, None] * j[None, :]) / (LOW * LANES)
    twiddle = np.stack([np.cos(twist), np.sin(twist)]).astype(np.float32)
    m = np.arange(LOW)[:, None, None] + np.arange(WINDOW)[:, None]
    last_angle = 2 * math.pi * ((m * low) % LOW) / LOW
    last = np.concatenate([np.cos(last_angle), -np.sin(last_angle)], -1)
    last_high, last_low = (t.astype(np.float32) for t in numpy_halves(last))
    last_all = np.concatenate([last_high, last_low, last_high], -1)
    return np.concatenate([first_high, first_high, first_low], 0), twiddle, last_all


def pack_kernel(spectrum_ref, out_ref, got, packed, sems):
    groups, dests = 4, out_ref.shape[0]
    count = dests // groups
    heads = [
        pltpu.make_async_copy(
            spectrum_ref.at[:, pl.ds(4 * count * group, 4 * count), :],
            got.at[:, pl.ds(4 * count * group, 4 * count), :],
            sems.at[group],
        )
        for group in range(groups)
    ]
    tails = [
        pltpu.make_async_copy(
            packed.at[pl.ds(count * group, count)],
            out_ref.at[pl.ds(count * group, count)],
            sems.at[groups + group],
        )
        for group in range(groups)
    ]
    for copy in heads:
        copy.start()
    for group in range(groups):
        heads[group].wait()
        for dest in range(count * group, count * (group + 1)):
            for part in range(6):
                packed[dest, 4 * part : 4 * part + 4, :] = got[part, 4 * dest : 4 * dest + 4, :]
        tails[group].start()
    for copy in tails:
        copy.wait()


def edges_of(theta_ref):
    spot = lax.broadcasted_iota(jnp.int32, (8, LANES), 1)
    edges = jnp.zeros((8, LANES), jnp.float32)
    cells = theta_ref.shape[2]
    for z in range(4):
        tail = pltpu.roll(theta_ref[:, z, cells - LANES :], (8 * z + 4) % LANES, 1)
        head = pltpu.roll(theta_ref[:, z, :LANES], 8 * z + 4, 1)
        edges = jnp.where((spot >= 8 * z) & (spot < 8 * z + 4), tail, edges)
        edges = jnp.where((spot >= 8 * z + 4) & (spot < 8 * z + 8), head, edges)
    return edges


def setup_kernel(
    offset_hbm, theta_in, last, first_in, twiddle_in,
    left_ref, turn_ref, edges_ref, first_ref, twiddle_ref, theta, y_first_ref, y_last_ref,
    offset, sems,
):
    copy = pltpu.make_async_copy(offset_hbm, offset, sems.at[0])
    copy.start()
    theta[...] = theta_in[...]
    y_first_ref[...] = theta_in[:4]
    y_last_ref[...] = theta_in[theta_in.shape[0] - 4 :]
    first_ref[...] = first_in[...]
    twiddle_ref[...] = twiddle_in[...]
    edges_ref[...] = edges_of(theta_in)
    copy.wait()
    blocks = left_ref.shape[0] // WINDOW
    left = [last[offset[block] // LANES] for block in range(blocks)]
    left_ref[...] = jnp.concatenate(left, 0).astype(jnp.bfloat16)
    lane = lax.broadcasted_iota(jnp.int32, (1, LANES), 1)
    for block in range(blocks):
        turn_ref[block : block + 1, :] = jnp.where(lane < offset[block] % LANES, 1.0, 0.0)


def matrix_kernel(
    near, offset_hbm, length_hbm, index_ref, weight_ref, after_ref, *outs_and_scratch
):
    count = PAIRS
    refs, far_hbms = outs_and_scratch[:near], outs_and_scratch[near:count]
    offset, length = outs_and_scratch[count : count + 2]
    refs = refs + outs_and_scratch[count + 2 : -2]
    sems, out_sems = outs_and_scratch[-2:]
    block = lax.axis_index("gx")
    cells = index_ref.shape[1] // lax.axis_size("gx")
    first_cell = block * cells
    heads = [
        pltpu.make_async_copy(source, target, sems.at[number])
        for number, (source, target) in enumerate(((offset_hbm, offset), (length_hbm, length)))
    ]
    for copy in heads:
        copy.start()
    for copy in heads:
        copy.wait()
    start, live = offset[block], length[block]
    rows = lax.broadcasted_iota(jnp.int32, (8, LANES), 0)
    taps = index_ref.shape[0]
    copies = []
    for number in range(PAIRS):
        pair = (number + near) % PAIRS
        matrix = refs[pair]
        for side in range(2):
            lanes = pl.ds(pl.multiple_of(first_cell + (2 * pair + side) * LANES, LANES), LANES)
            index = index_ref[:, lanes]
            weight = jnp.where(index < live, weight_ref[:, lanes], 0.0)
            inner = lax.rem(index + start, LANES)
            spots = [jnp.broadcast_to(inner[t : t + 1], (8, LANES)) for t in range(taps)]
            parts = []
            for m in range(SEGMENT):
                part = jnp.where(index // LANES == m, weight, 0.0)
                parts.append([jnp.broadcast_to(part[t : t + 1], (8, LANES)) for t in range(taps)])

            def step(number, carry, side=side, matrix=matrix, spots=spots, parts=parts):
                sums = []
                for half in range(2):
                    near = rows + (16 * number + 8 * half)
                    hits = [near == spots[t] for t in range(taps)]
                    for m in range(SEGMENT):
                        total = jnp.where(hits[0], parts[m][0], 0.0)
                        for t in range(1, taps):
                            total = jnp.where(hits[t], total + parts[m][t], total)
                        sums.append(total)
                for m in range(SEGMENT):
                    high, low = halves(jnp.concatenate([sums[m], sums[SEGMENT + m]], 0))
                    at = pl.ds(pl.multiple_of(LANES * m + 16 * number, 16), 16)
                    matrix[0, at, side * LANES : (side + 1) * LANES] = high
                    matrix[1, at, side * LANES : (side + 1) * LANES] = low
                return carry

            lax.fori_loop(0, LANES // 16, step, 0)
        if pair >= near:
            copies.append(
                pltpu.make_async_copy(matrix, far_hbms[pair - near], out_sems.at[pair - near])
            )
            copies[-1].start()
    for copy in copies:
        copy.wait()


def transform_kernel(
    got_ref, first_ref, twiddle_ref, left_ref, turn_ref, edges_ref, *after_and_out
):
    out_ref = after_and_out[-1]
    lane = lax.broadcasted_iota(jnp.int32, (LOW, LANES), 1) // LOW
    pieces = []
    for comp in range(3):
        rows = [
            got_ref[pl.ds(comp * 8 + part * 4 + z, 16, stride=24), :]
            for z in range(4)
            for part in range(2)
        ]
        turned = jnp.concatenate(rows, 0).T
        for z in range(4):
            piece = jnp.zeros((LOW, LANES), jnp.float32)
            for h in range(4):
                moved = turned[LOW * h : LOW * (h + 1), :]
                if h != z:
                    moved = pltpu.roll(moved, (LOW * (h - z)) % LANES, 1)
                piece = jnp.where(lane == h, moved, piece)
            pieces.append(piece)
    high, low = halves(jnp.concatenate(pieces, 0))
    done = dot(jnp.concatenate([high, low], 1), first_ref[: 2 * LANES, :]) + dot(
        high, first_ref[2 * LANES :, :]
    )
    cosine, sine = twiddle_ref[0], twiddle_ref[1]
    right = []
    for line in range(12):
        real = done[LOW * line : LOW * (line + 1), :LANES]
        imag = done[LOW * line : LOW * (line + 1), LANES:]
        high, low = halves(
            jnp.concatenate([real * cosine - imag * sine, real * sine + imag * cosine], 0)
        )
        right.append(jnp.concatenate([high, high, low], 0))
    lines = dot(left_ref[...], jnp.concatenate(right, 1))
    for block in range(out_ref.shape[0]):
        turned = jnp.broadcast_to(turn_ref[block : block + 1, :], (WINDOW, LANES)) > 0.5
        for line in range(12):
            cells = lines[WINDOW * block : WINDOW * (block + 1), line * LANES : (line + 1) * LANES]
            out_ref[block, line] = jnp.where(turned, pltpu.roll(cells, WINDOW - 1, 0), cells)
    for block in range(out_ref.shape[0]):
        for y in range(8):
            out_ref[block, y, WINDOW - 1 :, :] = edges_ref[y : y + 1]


def stencil_kernel(
    z_low_ref, z_high_ref, y_low_ref, y_high_ref, theta_ref, sum_ref, after_ref,
    local_hbm,
    local_ref, sems,
):
    cells = theta_ref.shape[2]
    lane = lax.broadcasted_iota(jnp.int32, (8, cells), 1)
    planes = [ref[:, z, :] for ref in (z_low_ref, theta_ref, z_high_ref) for z in range(4)]
    for z in range(4):
        here = planes[4 + z]
        column = jnp.concatenate([y_low_ref[:, z, :], here, y_high_ref[:, z, :]], 0)
        grad_x = jnp.zeros_like(here)
        grad_y = jnp.zeros_like(here)
        grad_z = jnp.zeros_like(here)
        laplace = 3.0 * center_coeff * here
        for reach in range(1, 5):
            first = -time_step * first_coeffs[reach - 1]
            ahead_x = jnp.where(lane < cells - reach, pltpu.roll(here, cells - reach, 1), 0.0)
            behind_x = jnp.where(lane >= reach, pltpu.roll(here, reach, 1), 0.0)
            ahead_y = column[4 + reach : 12 + reach]
            behind_y = column[4 - reach : 12 - reach]
            ahead_z = planes[4 + z + reach]
            behind_z = planes[4 + z - reach]
            grad_x = grad_x + first * (ahead_x - behind_x)
            grad_y = grad_y + first * (ahead_y - behind_y)
            grad_z = grad_z + first * (ahead_z - behind_z)
            laplace = laplace + second_coeffs[reach - 1] * (
                (ahead_x + behind_x) + (ahead_y + behind_y) + (ahead_z + behind_z)
            )
        local_ref[0, z] = grad_x
        local_ref[1, z] = grad_y
        local_ref[2, z] = grad_z
        local_ref[3, z] = section_keep * sum_ref[:, z, :] + (time_step * diffusivity) * laplace
        local_ref[4, z] = here
    copy = pltpu.make_async_copy(local_ref, local_hbm, sems.at[0])
    copy.start()
    copy.wait()


def combine_kernel(near, got_ref, local_hbm, *refs):
    matrices, far_hbms = refs[:near] + refs[PAIRS + 2 : -2], refs[near:PAIRS]
    theta_ref, section_ref = refs[PAIRS : PAIRS + 2]
    local_ref, sems = refs[-2:]
    moves = list(zip(far_hbms, matrices[near:], strict=True)) + [(local_hbm, local_ref)]
    copies = [
        pltpu.make_async_copy(source, target, sems.at[number])
        for number, (source, target) in enumerate(moves)
    ]
    for copy in copies:
        copy.start()
    block = lax.axis_index("gx")
    blocks = got_ref.shape[0] // (12 * WINDOW)
    cells = local_ref.shape[3]
    rows = [
        jnp.concatenate(
            [
                got_ref[pl.ds(WINDOW * line + m, blocks, stride=12 * WINDOW), :]
                for line in range(12)
            ],
            0,
        )
        for m in range(SEGMENT)
    ]
    high, low = halves(jnp.concatenate(rows, 1))
    both = jnp.concatenate([high, low], 0)
    count = high.shape[0]

    def halo_of(source):
        return got_ref[pl.ds(source * 12 * WINDOW + WINDOW - 1, 8, stride=WINDOW), :]

    before = halo_of(lax.rem(block + blocks - 1, blocks))
    after = halo_of(lax.rem(block + 1, blocks))
    lane = lax.broadcasted_iota(jnp.int32, (8, LANES), 1)
    width = 2 * LANES
    carried_of = []
    for tile in range(cells // width):
        if tile >= near:
            copies[tile - near].wait()
        twice = dot(both, matrices[tile][0])
        carried_of.append(twice[:count] + twice[count:] + dot(high, matrices[tile][1]))
    copies[-1].wait()
    for tile in range(cells // width):
        lanes = slice(tile * width, (tile + 1) * width)
        carried = carried_of[tile]
        for z in range(4):
            grad_x = local_ref[0, z, :, lanes]
            base = local_ref[3, z, :, lanes]
            if tile == 0 or (tile + 1) * width == cells:
                more_grad = jnp.zeros((8, LANES), jnp.float32)
                more_base = jnp.zeros((8, LANES), jnp.float32)
                for reach in range(1, 5):
                    if tile == 0:
                        moved = pltpu.roll(before, (LANES - 4 - 8 * z + reach) % LANES, 1)
                        halo = jnp.where(lane < reach, moved, 0.0)
                        sign = 1.0
                    else:
                        moved = pltpu.roll(after, (LANES - 4 - 8 * z - reach) % LANES, 1)
                        halo = jnp.where(lane >= LANES - reach, moved, 0.0)
                        sign = -1.0
                    more_grad = more_grad + (sign * time_step * first_coeffs[reach - 1]) * halo
                    more_base = (
                        more_base + (time_step * diffusivity * second_coeffs[reach - 1]) * halo
                    )
                none = jnp.zeros((8, LANES), jnp.float32)
                order = (lambda v: [v, none]) if tile == 0 else (lambda v: [none, v])
                grad_x = grad_x + jnp.concatenate(order(more_grad), 1)
                base = base + jnp.concatenate(order(more_base), 1)
            section = (
                base
                + carried[8 * z : 8 * z + 8] * grad_x
                + carried[32 + 8 * z : 40 + 8 * z] * local_ref[1, z, :, lanes]
                + carried[64 + 8 * z : 72 + 8 * z] * local_ref[2, z, :, lanes]
            )
            section_ref[:, z, lanes] = section
            theta_ref[:, z, lanes] = local_ref[4, z, :, lanes] + section_gain * section


def f32(*shape):
    return jax.ShapeDtypeStruct(shape, jnp.float32)


def bf16(*shape):
    return jax.ShapeDtypeStruct(shape, jnp.bfloat16)


VMEM = pl.BlockSpec(memory_space=pltpu.VMEM)
HBM = pl.BlockSpec(memory_space=pltpu.HBM)
ANY = pl.BlockSpec(memory_space=pl.ANY)


def in_hbm(array):
    return pltpu.with_memory_space_constraint(array, pltpu.HBM)


def run(kernel, name, in_specs, outs, scratch=()):
    return pl.pallas_call(
        kernel,
        out_shape=tuple(shape for shape, _ in outs),
        in_specs=in_specs,
        out_specs=tuple(spec for _, spec in outs),
        scratch_shapes=scratch,
        compiler_params=pltpu.CompilerParams(vmem_limit_bytes=VMEM_LIMIT),
        cost_estimate=pl.CostEstimate(flops=4 * 10**9, bytes_accessed=4 * 10**6, transcendentals=0),
        name=name,
    )


def neighbours(edge_low, edge_high, axis):
    count = lax.axis_size(axis)
    up = [(i, (i + 1) % count) for i in range(count)]
    return lax.ppermute(edge_high, axis, up), lax.ppermute(edge_low, axis, [(b, a) for a, b in up])


def body(spectrum, theta, section_sum, seg_offset, seg_length, stencil_index, stencil_weight):
    blocks, depth = lax.axis_size("gx"), lax.axis_size("gz")
    rows_count, layers, cells = theta.shape
    first, twiddle, last = (jnp.asarray(t) for t in tables())
    vmem, smem, dma = pltpu.VMEM, pltpu.SMEM, pltpu.SemaphoreType.DMA

    edge = f32(4, layers, cells)
    (packed,) = run(
        pack_kernel,
        "pack",
        [HBM],
        [(f32(depth, 24, LANES), HBM)],
        [vmem((6, 4 * depth, LANES), jnp.float32), vmem((depth, 24, LANES), jnp.float32), dma((8,))],
    )(in_hbm(spectrum.reshape(6, 4 * depth, LANES)))
    columns = lax.all_to_all(packed, "gz", split_axis=0, concat_axis=0, tiled=True)
    left, turn, edges, first, twiddle, copied, y_first, y_last = run(
        setup_kernel,
        "setup",
        [HBM] + [VMEM] * 4,
        [
            (bf16(blocks * WINDOW, last.shape[2]), VMEM),
            (f32(blocks, LANES), VMEM),
            (f32(8, LANES), VMEM),
            (bf16(*first.shape), VMEM),
            (f32(*twiddle.shape), VMEM),
            (f32(*theta.shape), VMEM),
            (edge, VMEM),
            (edge, VMEM),
        ],
        [smem((blocks,), jnp.int32), dma((1,))],
    )(seg_offset, theta, last, first, twiddle)
    y_low, y_high = neighbours(y_first, y_last, "gy")
    z_low, z_high = neighbours(copied, copied, "gz")
    (pieces,) = run(
        transform_kernel,
        "transform",
        [VMEM] * 6,
        [(f32(blocks, 12, WINDOW, LANES), VMEM)],
    )(columns.reshape(depth * 24, LANES), first, twiddle, left, turn, edges)
    arrived = lax.all_to_all(pieces, "gx", split_axis=0, concat_axis=0, tiled=True)
    part = (2, SEGMENT * LANES, cells // PAIRS)
    far_parts = [vmem(part, jnp.bfloat16)] * (PAIRS - NEAR)
    matrices = run(
        functools.partial(matrix_kernel, NEAR),
        "matrix",
        [HBM, HBM, VMEM, VMEM, ANY],
        [(bf16(*part), VMEM)] * NEAR + [(pltpu.HBM(part, jnp.bfloat16), HBM)] * (PAIRS - NEAR),
        [smem((blocks,), jnp.int32), smem((blocks,), jnp.int32)]
        + far_parts
        + [dma((2,)), dma((PAIRS,))],
    )(seg_offset, seg_length, stencil_index, stencil_weight, pieces)
    matrices = matrices[:NEAR] + tuple(in_hbm(far) for far in matrices[NEAR:])
    local_shape = (5, layers, rows_count, cells)
    (local,) = run(
        stencil_kernel,
        "stencil",
        [VMEM] * 6 + [ANY],
        [(pltpu.HBM(local_shape, jnp.float32), HBM)],
        [vmem(local_shape, jnp.float32), dma((1,))],
    )(z_low, z_high, y_low, y_high, theta, section_sum, pieces)
    return run(
        functools.partial(combine_kernel, NEAR),
        "combine",
        [VMEM, HBM] + [VMEM] * NEAR + [HBM] * (PAIRS - NEAR),
        [(f32(*theta.shape), VMEM), (f32(*theta.shape), VMEM)],
        far_parts + [vmem(local_shape, jnp.float32), dma((PAIRS + 1,))],
    )(arrived.reshape(blocks * 12 * WINDOW, LANES), in_hbm(local), *matrices)


def solution(mesh):
    placed = (
        P(None, None, ("gy", "gx"), None, "gz"),
        P("gy", "gz", "gx"),
        P("gy", "gz", "gx"),
        P(),
        P(),
        P(),
        P(),
    )
    return jax.shard_map(
        body,
        mesh=mesh,
        in_specs=placed,
        out_specs=(P("gy", "gz", "gx"), P("gy", "gz", "gx")),
        check_vma=False,
    )
```
